32 devices in a mesh: src: 8 (over z, core), freq: 4 (over y, x).
Axes of the slice: x: 2, y: 2, z: 4, core: 2. Of those that a mesh axis runs over, the one named last changes fastest.
Arguments:
- weights: bfloat16 [512, 512, 128], P('src', 'freq'), may hold values from -6 to 6
- kernels: bfloat16 [4, 2, 2, 128, 128], replicated, as said below
- src_phase: float32 [4, 64, 512], replicated, may hold values from -3.140625 to 3.140625
- freq_phase: float32 [4, 64, 512], replicated, may hold values from 0.5 to 4
Outputs:
- result: bfloat16 [512, 512, 128], P(('src', 'freq'))
The draws below stay inside these ranges and needn't reach their ends.
Inputs may be any that keep to these rules, and one draw needn't show every extreme that they name: Every kernels[l, b, c] has the form [[A, B], [-B, A]] with 64 x 64 blocks A and B.
All inputs are finite; a program needn't handle non-finite values.
Results may differ from the reference program's by a relative error of at most 0.0064.
Values may be sent and summed in bfloat16 or wider, within the bound.
No kernel may reach another device: no remote copies, remote signals or barrier semaphores. Data moves between devices by JAX's collectives and lax.ppermute only.
A program may use at most 128 MiB of HBM per device.

```python
import math
import jax
import jax.numpy as jnp
from jax import lax

S_DEV = 64
F_DEV = 128
PTS = 64
COMP = 128
LEVELS = 4
SRC_BOXES = 512
FREQ_BOXES = 512
N_SRC = 8
N_FREQ = 4


def draw_kernels(key, part):
    key = jax.random.fold_in(key, 5)
    key_real, key_imag = jax.random.split(key)
    shape = (LEVELS, 2, 2, PTS, PTS)
    scale = (2.0 * COMP) ** (-0.5)
    real_part = jax.random.truncated_normal(key_real, -6.0, 6.0, shape, jnp.float32) * scale
    imag_part = jax.random.truncated_normal(key_imag, -6.0, 6.0, shape, jnp.float32) * scale
    upper = jnp.concatenate([real_part, imag_part], -1)
    lower = jnp.concatenate([-imag_part, real_part], -1)
    return jnp.concatenate([upper, lower], -2).astype(jnp.bfloat16)


def steps_of(key, dims, pieces, low, largest):
    gain = 1.0
    for axis_at, blocks in pieces:
        heights = jax.random.uniform(jax.random.fold_in(jax.random.fold_in(key, 6), axis_at), (blocks,), jnp.float32, low / len(pieces), largest / len(pieces))
        gain = gain * jnp.repeat(jnp.exp(heights), dims[axis_at] // blocks).reshape((-1,) + (1,) * (len(dims) - 1 - axis_at))
    return gain


def noise(own_key, dims, spread, reach, cuts=(), held_as=jnp.bfloat16):
    array = spread * jax.random.normal(own_key, dims, jnp.float32)
    if cuts:
        array = array * steps_of(own_key, dims, cuts, -0.22, 0.18)
    return jnp.clip(array, -reach, reach).astype(held_as)


def setup_inputs(seed: int = 0) -> dict:
    seeds = jax.random.split(jax.random.key(seed), 5)
    weights = noise(seeds[0], (SRC_BOXES, FREQ_BOXES, COMP), 1.0, 6.0, ((0, 8), (1, 4)))
    kernels = draw_kernels(jax.random.fold_in(seeds[4], 71), 0)
    src_phase = jnp.clip(jax.random.uniform(seeds[2], (LEVELS, PTS, SRC_BOXES), jnp.float32, -3.140625, 3.140625), -3.140625, 3.140625)
    freq_phase = jnp.clip(jnp.exp(jax.random.uniform(seeds[3], (LEVELS, PTS, FREQ_BOXES), jnp.float32, math.log(0.5), math.log(4.0))), 0.5, 4.0)
    return {"weights": weights, "kernels": kernels, "src_phase": src_phase, "freq_phase": freq_phase}


def mix(lower, upper, kern):
    shape = lower.shape
    width = shape[-1]
    low2 = lower.reshape(-1, width)
    up2 = upper.reshape(-1, width)
    first = jnp.dot(low2, kern[0, 0], preferred_element_type=jnp.float32) + jnp.dot(up2, kern[0, 1], preferred_element_type=jnp.float32)
    second = jnp.dot(low2, kern[1, 0], preferred_element_type=jnp.float32) + jnp.dot(up2, kern[1, 1], preferred_element_type=jnp.float32)
    return first.reshape(shape), second.reshape(shape)


def phase_part(phase, start, count):
    piece = lax.dynamic_slice_in_dim(phase, start, count, 1)
    return jnp.concatenate([piece, piece], 0).T


def rotate(values, angle):
    half = values.shape[-1] // 2
    flipped = jnp.concatenate([-values[..., half:], values[..., :half]], -1)
    return (values * jnp.cos(angle) + flipped * jnp.sin(angle)).astype(jnp.bfloat16)


def level_rows(block, kern, row_angle, col_angle, step):
    count, cols, width = block.shape
    grouped = block.reshape(count // (2 * step), 2, step, cols, width)
    first, second = mix(grouped[:, 0], grouped[:, 1], kern)
    mixed = jnp.stack([first, second], 1).reshape(count, cols, width)
    return rotate(mixed, row_angle[:, None, :] * col_angle[None, :, :])


def level_cols(block, kern, row_angle, col_angle):
    count, cols, width = block.shape
    grouped = block.reshape(count, 2, cols // 2, width)
    first, second = mix(grouped[:, 0], grouped[:, 1], kern)
    mixed = jnp.stack([first, second], 1).reshape(count, cols, width)
    return rotate(mixed, row_angle[:, None, :] * col_angle[None, :, :])


def reference(weights, kernels, src_phase, freq_phase):
    state = weights
    bits = N_SRC.bit_length() - 1
    for level in range(3):
        step = S_DEV * 2 ** (bits - 1 - level)
        row_angle = phase_part(src_phase[level], 0, SRC_BOXES)

        def column_block(index, level=level, step=step, state=state, row_angle=row_angle):
            start = index * F_DEV
            block = lax.dynamic_slice_in_dim(state, start, F_DEV, 1)
            col_angle = phase_part(freq_phase[level], start, F_DEV)
            return level_rows(block, kernels[level], row_angle, col_angle, step)

        blocks = lax.map(column_block, jnp.arange(N_FREQ, dtype=jnp.int32))
        state = jnp.moveaxis(blocks, 0, 1).reshape(SRC_BOXES, FREQ_BOXES, COMP)
    col_angle = phase_part(freq_phase[3], 0, FREQ_BOXES)

    def row_block(index):
        start = index * S_DEV
        block = lax.dynamic_slice_in_dim(state, start, S_DEV, 0)
        row_angle = phase_part(src_phase[3], start, S_DEV)
        return level_cols(block, kernels[3], row_angle, col_angle)

    blocks = lax.map(row_block, jnp.arange(N_SRC, dtype=jnp.int32))
    return blocks.reshape(SRC_BOXES, FREQ_BOXES, COMP)
```

```python
import functools

import jax
import jax.numpy as jnp
from jax import lax
from jax.experimental import pallas as pl
from jax.experimental.pallas import tpu as pltpu
from jax.sharding import PartitionSpec as P

SIN = (4.44288292, -7.3082457, 3.60635441, -0.84611289, 0.10982699)
COS = (1.4142135, -6.97885099, 5.73946117, -1.88356299, 0.31069819)
NEAREST = 12582912.0
FIRST = 48
VMEM = 48 * 2**20


def swapped(block, axis, mask):
    count = lax.axis_size(axis)
    return lax.ppermute(block, axis, [(at, at ^ mask) for at in range(count)])


def after(value, *earlier):
    return lax.optimization_barrier((value, *earlier))[0]


def turned(u, v, turns):
    part = turns - ((turns + NEAREST) - NEAREST)
    square = part * part
    sine, cosine = SIN[-1], COS[-1]
    for term in SIN[-2::-1]:
        sine = sine * square + term
    for term in COS[-2::-1]:
        cosine = cosine * square + term
    sine = sine * part
    cosine, sine = 1.0 - sine * sine, sine * cosine
    return u * cosine - v * sine, v * cosine + u * sine


def halves(y, turns):
    return turned(y[:, :128], y[:, 128:], turns)


def packed(y, turns):
    u, v = halves(y, turns)
    return jnp.concatenate([u, v], -1).astype(jnp.bfloat16)


def product(left, right, kern):
    return jnp.dot(jnp.concatenate([left, right], -1), kern, preferred_element_type=jnp.float32)


def split_pairs(y, turns):
    u, v = halves(y, turns)
    low = lax.broadcasted_iota(jnp.int32, u.shape, 1) < u.shape[1] // 2
    half = u.shape[1] // 2
    even = jnp.where(low, u, pltpu.roll(v, half, 1))
    odd = jnp.where(low, pltpu.roll(u, half, 1), v)
    return even.astype(jnp.bfloat16), odd.astype(jnp.bfloat16)


def first_levels(low, count, at, x0, x1, x2, x3, kern0, kern1, src, freq, out):
    x = (x0, x1, x2, x3)
    pairs = out.shape[2]
    rows = pairs * count
    turns = [freq[level, 0, low : low + count] for level in range(2)]

    def raw(block):
        both = block[0].reshape(pairs, 2, count, 128)
        return jnp.concatenate([both[:, 0].reshape(rows, 128), both[:, 1].reshape(rows, 128)], -1)

    left = jnp.concatenate([raw(x[0]), raw(x[1])], 0)
    right = jnp.concatenate([raw(x[2]), raw(x[3])], 0)
    mid = [[None, None], [None, None]]
    for b0 in range(2):
        y = product(left, right, kern0[b0])
        for b1 in range(2):
            mid[b0][b1] = jnp.concatenate(
                [
                    packed(
                        y[b1 * rows + p * count : b1 * rows + (p + 1) * count],
                        src[0, 2 * b0 + b1, 0, p : p + 1] * turns[0],
                    )
                    for p in range(pairs)
                ],
                0,
            )
    left = jnp.concatenate([mid[0][0], mid[1][0]], 0)
    right = jnp.concatenate([mid[0][1], mid[1][1]], 0)
    for b1 in range(2):
        y = product(left, right, kern1[b1])
        for b0 in range(2):
            for p in range(pairs):
                out[2 * b0 + b1, 0, p] = packed(
                    y[b0 * rows + p * count : b0 * rows + (p + 1) * count],
                    src[1, 2 * b0 + b1, 0, p : p + 1] * turns[1],
                )


def third_level(low, count, at, own, other, kern, src, freq, *outs):
    parts = len(outs)
    pairs = own.shape[2]
    here = at[0]
    turns = freq[2, here, low : low + count]
    for q in range(parts):
        to = here ^ q
        y = product(
            own[:, to].reshape(4 * pairs * count, 256), other[:, to].reshape(4 * pairs * count, 256), kern[...]
        )
        for k in range(4):
            for p in range(pairs):
                at_row = (k * pairs + p) * count
                outs[q][k, p] = packed(y[at_row : at_row + count], src[2, k, to, p : p + 1] * turns)


def last_level(low, count, here, x, kern, src, freq, outs):
    parts = len(x)
    pairs = x[0].shape[1]
    for q in range(parts // 2):
        left = x[q][...].reshape(4 * pairs * count, 256)
        right = x[q + parts // 2][...].reshape(4 * pairs * count, 256)
        for b in range(2):
            to = here ^ (q + b * (parts // 2))
            turns = freq[3, to, low : low + count]
            y = product(left, right, kern[b])
            for k in range(4):
                for p in range(pairs):
                    at_row = (k * pairs + p) * count
                    even, odd = split_pairs(y[at_row : at_row + count], src[3, k, here, p : p + 1] * turns)
                    outs[k][2 * p, to] = even
                    outs[k][2 * p + 1, to] = odd


def fourth_level(low, count, parts, at, *refs):
    x, (kern, src, freq), outs = refs[:parts], refs[parts : parts + 3], refs[parts + 3 :]
    last_level(low, count, at[0], x, kern, src, freq, outs)


def last_levels(low, count, parts, at, own, other, kern2, kern3, src, freq, *refs):
    outs, held = refs[:4], refs[4:]
    pairs = own.shape[2]
    here = at[0]
    for q in range(parts):
        turns = freq[2, here ^ q, low : low + count]
        y = product(
            own[:, q].reshape(4 * pairs * count, 256), other[:, q].reshape(4 * pairs * count, 256), kern2[...]
        )
        for k in range(4):
            for p in range(pairs):
                at_row = (k * pairs + p) * count
                held[q][k, p] = packed(y[at_row : at_row + count], src[2, k, here, p : p + 1] * turns)
    last_level(low, count, here, held, kern3, src, freq, outs)


def gather(spans, at, *refs):
    count = 4 * len(spans)
    parts, out, sems = refs[:count], refs[count], refs[count + 1]
    copies = []
    for c, (low, size) in enumerate(spans):
        for k in range(4):
            n = 4 * c + k
            copies.append(
                pltpu.make_async_copy(parts[n], out.at[at[0] ^ k, :, :, pl.ds(low, size)], sems.at[n])
            )
    for copy in copies:
        copy.start()
    for copy in copies:
        copy.wait()


def whole(shape):
    return pl.BlockSpec(shape, lambda *_: (0,) * len(shape))


def call(kernel, at, operands, outs, scratch=(), grid=(), in_specs=None, out_specs=None, flops=0):
    return pl.pallas_call(
        kernel,
        out_shape=outs,
        grid_spec=pltpu.PrefetchScalarGridSpec(
            num_scalar_prefetch=1,
            grid=grid,
            in_specs=in_specs or [whole(x.shape) for x in operands],
            out_specs=out_specs or [whole(x.shape) for x in outs],
            scratch_shapes=list(scratch),
        ),
        compiler_params=pltpu.CompilerParams(vmem_limit_bytes=VMEM),
        cost_estimate=pl.CostEstimate(
            flops=flops,
            bytes_accessed=sum(x.size * x.dtype.itemsize for x in [*operands, *outs]),
            transcendentals=0,
        ),
    )(at, *operands)


def paired(kern, raw):
    parts = kern.reshape(*kern.shape[:-2], 2, 64, 2, 64)
    eye = jnp.eye(2, dtype=kern.dtype)
    form = "...apbq,st->...saptbq" if raw else "...apbq,st->...aspbtq"
    wide = jnp.einsum("...apbq,st->...sapbtq" if raw else "...apbq,st->...aspbtq", parts, eye)
    return wide.reshape(*kern.shape[:-2], 256, 256)


def flipped(kern, bit):
    turned_kern = jnp.where(bit == 1, kern[::-1, ::-1], kern)
    return turned_kern.reshape(2, 512, 256)


def body(weights, kernels, src_phase, freq_phase):
    n_src, n_freq = lax.axis_size("src"), lax.axis_size("freq")
    src_index, here = lax.axis_index("src"), lax.axis_index("freq")
    s_dev, f_dev, _ = weights.shape
    bits = n_src.bit_length() - 1
    shift = bits - 2
    chip = src_index >> shift
    rest = src_index & ((1 << shift) - 1)
    side = src_index >> (shift - 1) & 1
    near = s_dev // n_freq
    each = near // 4
    pairs = each // 2
    spans = ((0, FIRST), (FIRST, f_dev - FIRST))
    at = jnp.reshape(here, (1,)).astype(jnp.int32)
    bf16 = jnp.bfloat16

    raw = weights.reshape(n_freq, 4, each, f_dev, 128)

    def to_chip(k, span):
        return lax.dynamic_index_in_dim(raw, chip ^ k, 1, False)[:, :, span[0] : span[0] + span[1]]

    def over_chips(parts, *earlier):
        return [swapped(after(parts[k], *earlier), "src", k << shift) for k in (3, 2, 1)]

    out_a = [to_chip(k, spans[0]) for k in range(4)]
    a3 = swapped(out_a[3], "src", 3 << shift)
    a2 = swapped(out_a[2], "src", 2 << shift)
    a1 = swapped(out_a[1], "src", 1 << shift)

    low, count = spans[1]
    parts_b = [
        lax.dynamic_index_in_dim(raw, here ^ q, 0, False)[:, :, low : low + count] for q in range(n_freq)
    ]
    moved = [parts_b[0]] + [swapped(parts_b[q], "freq", q) for q in range(1, n_freq)]

    def to_chip_b(k):
        return jnp.stack([lax.dynamic_index_in_dim(x, chip ^ k, 0, False) for x in moved], 0)

    turn = 1.0 / (2.0 * jnp.pi)
    src = src_phase.reshape(4, 64, 4, 1 << shift, n_freq, 4, each)
    src = lax.dynamic_index_in_dim(src, rest, 3, False)
    src = lax.dynamic_index_in_dim(src, chip, 4, False)
    src = jnp.stack([lax.dynamic_index_in_dim(src, chip ^ k, 2, False) for k in range(4)], 2)
    src = src.transpose(0, 2, 3, 4, 1).reshape(4, 4, n_freq, pairs, 128) * turn
    freq = freq_phase.transpose(0, 2, 1).reshape(4, n_freq, f_dev, 64)
    freq = jnp.concatenate([freq, freq], -1)
    wide0 = flipped(paired(kernels[0], True), chip >> 1)
    wide1 = flipped(paired(kernels[1], False), chip & 1)
    wide2 = paired(lax.dynamic_index_in_dim(kernels[2], side, 0, False), False)
    wide2 = jnp.where(side == 1, wide2[::-1], wide2).reshape(512, 256)
    wide3 = flipped(paired(kernels[3], False), here // (n_freq // 2))

    def levels01(x, span, early):
        low, count = span
        prefetch = jnp.concatenate([at, jnp.arange(n_freq, dtype=jnp.int32) ^ (at if early else 0)])
        src_spec = pl.BlockSpec(
            (2, 4, 1, pairs, 128),
            (lambda m, s: (0, 0, s[0], 0, 0)) if early else (lambda m, s: (0, 0, m, 0, 0)),
        )
        freq_spec = pl.BlockSpec(
            (2, 1, f_dev, 128),
            (lambda m, s: (0, s[1 + m], 0, 0)) if early else (lambda m, s: (0, s[0], 0, 0)),
        )
        x_spec = pl.BlockSpec((1, each, count, 128), lambda m, s: (m, 0, 0, 0))
        rows = 4 * n_freq * pairs * count
        return call(
            functools.partial(first_levels, low, count),
            prefetch,
            [*x, wide0, wide1, src, freq],
            [jax.ShapeDtypeStruct((4, n_freq, pairs, count, 256), bf16)],
            grid=(n_freq,),
            in_specs=[x_spec] * 4 + [whole(wide0.shape), whole(wide1.shape), src_spec, freq_spec],
            out_specs=[pl.BlockSpec((4, 1, pairs, count, 256), lambda m, s: (0, m, 0, 0, 0))],
            flops=2 * 2 * rows * 512 * 256,
        )[0]

    def back_shapes(count):
        return [jax.ShapeDtypeStruct((each, n_freq, count, 128), bf16)] * 4

    out_b = [to_chip_b(k) for k in range(4)]
    b3 = swapped(after(out_b[3], a3), "src", 3 << shift)
    b2 = swapped(after(out_b[2], a2), "src", 2 << shift)
    b1 = swapped(after(out_b[1], a1), "src", 1 << shift)

    low, count = spans[0]
    state_a = levels01([out_a[0], a1, a2, a3], spans[0], False)
    other_a = swapped(state_a, "src", 1 << (shift - 1))
    sent = call(
        functools.partial(third_level, low, count),
        at,
        [state_a, other_a, wide2, src, freq],
        [jax.ShapeDtypeStruct((4, pairs, count, 256), bf16)] * n_freq,
        flops=2 * 4 * n_freq * pairs * count * 512 * 256,
    )
    got = [sent[0]] + [swapped(sent[q], "freq", q) for q in range(1, n_freq)]
    back_a = call(
        functools.partial(fourth_level, low, count, n_freq),
        at,
        [*got, wide3, src, freq],
        back_shapes(count),
        flops=2 * 4 * n_freq * pairs * count * 512 * 256,
    )
    end_a = [None] * 4
    end_a[0] = back_a[0]
    for k, earlier in ((3, b3), (2, b2), (1, b1)):
        end_a[k] = swapped(after(back_a[k], earlier), "src", k << shift)

    low, count = spans[1]
    state_b = levels01([out_b[0], b1, b2, b3], spans[1], True)
    other_b = swapped(state_b, "src", 1 << (shift - 1))
    back_b = call(
        functools.partial(last_levels, low, count, n_freq),
        at,
        [state_b, other_b, wide2, wide3, src, freq],
        back_shapes(count),
        scratch=[pltpu.VMEM((4, pairs, count, 256), bf16)] * n_freq,
        flops=2 * 2 * 4 * n_freq * pairs * count * 512 * 256,
    )
    end_b = [None] * 4
    end_b[0] = back_b[0]
    for k in (3, 2, 1):
        end_b[k] = swapped(after(back_b[k], end_a[k]), "src", k << shift)

    ends = [*end_a, *end_b]
    out = call(
        functools.partial(gather, spans),
        jnp.reshape(chip, (1,)).astype(jnp.int32),
        ends,
        [jax.ShapeDtypeStruct((4, each, n_freq, f_dev, 128), bf16)],
        scratch=[pltpu.SemaphoreType.DMA((len(ends),))],
        in_specs=[pl.BlockSpec(memory_space=pl.ANY)] * len(ends),
        out_specs=[pl.BlockSpec(memory_space=pl.ANY)],
    )[0]
    return out.reshape(near, n_freq * f_dev, 128)


def solution(mesh):
    placed = (P("src", "freq", None), P(), P(), P())
    return jax.shard_map(
        body, mesh=mesh, in_specs=placed, out_specs=P(("src", "freq"), None, None), check_vma=False
    )
```

```python
import functools
import math

import jax
import jax.numpy as jnp
from jax import lax
from jax.experimental import pallas as pl
from jax.experimental.pallas import tpu as pltpu
from jax.sharding import PartitionSpec as P

SIN = (4.44288292, -7.3082457, 3.60635441, -0.84611289, 0.10982699)
COS = (1.4142135, -6.97885099, 5.73946117, -1.88356299, 0.31069819)
NEAREST = 12582912.0
FIRST = 64
VMEM = 48 * 2**20


def swapped(block, axis, mask):
    count = lax.axis_size(axis)
    return lax.ppermute(block, axis, [(at, at ^ mask) for at in range(count)])


def after(value, *earlier):
    return lax.optimization_barrier((value, *earlier))[0]


def turned(u, v, turns):
    part = turns - ((turns + NEAREST) - NEAREST)
    square = part * part
    sine, cosine = SIN[-1], COS[-1]
    for term in SIN[-2::-1]:
        sine = sine * square + term
    for term in COS[-2::-1]:
        cosine = cosine * square + term
    sine = sine * part
    cosine, sine = 1.0 - sine * sine, sine * cosine
    return u * cosine - v * sine, v * cosine + u * sine


def halves(y, turns):
    return turned(y[:, :128], y[:, 128:], turns)


def packed(y, turns):
    u, v = halves(y, turns)
    return jnp.concatenate([u, v], -1).astype(jnp.bfloat16)


def product(left, right, kern):
    return jnp.dot(jnp.concatenate([left, right], -1), kern, preferred_element_type=jnp.float32)


def split_pairs(y, turns):
    u, v = halves(y, turns)
    low = lax.broadcasted_iota(jnp.int32, u.shape, 1) < u.shape[1] // 2
    half = u.shape[1] // 2
    even = jnp.where(low, u, pltpu.roll(v, half, 1))
    odd = jnp.where(low, pltpu.roll(u, half, 1), v)
    return even.astype(jnp.bfloat16), odd.astype(jnp.bfloat16)


def prepare(at, src_in, freq_in, kern_in, src, freq, wide):
    turn = 1.0 / (2.0 * math.pi)
    lanes = lax.broadcasted_iota(jnp.int32, (128, 128), 1) < 64
    for level in range(4):
        rows = src_in[level].T * turn
        both = jnp.concatenate([rows, rows], -1)
        low = lax.broadcasted_iota(jnp.int32, both.shape, 1) < 64
        src[level] = jnp.where(low, both, pltpu.roll(both, both.shape[0] - 1, 0))
        rows = freq_in[level].T
        freq[level] = jnp.concatenate([rows, rows], -1)
        for b in range(2):
            for c in range(2):
                kern = kern_in[level, b ^ at[level], c ^ at[level]].astype(jnp.float32)
                over = pltpu.roll(kern, 64, 1)
                none = jnp.zeros_like(kern)
                forms = [
                    jnp.concatenate([jnp.where(lanes, kern, none), jnp.where(lanes, over, none)], -1),
                    jnp.concatenate([jnp.where(lanes, none, over), jnp.where(lanes, none, kern)], -1),
                ]
                for t in range(2):
                    form = forms[t].astype(jnp.bfloat16)
                    if level == 0:
                        wide[level, b, pl.ds(256 * c + 128 * t, 128)] = form
                    else:
                        for part in range(2):
                            wide[level, b, pl.ds(256 * c + 128 * part + 64 * t, 64)] = form[64 * part : 64 * part + 64]


def first_levels(low, count, early, at, x0, x1, x2, x3, kern0, kern1, src, freq, *outs):
    x = (x0, x1, x2, x3)
    pairs = outs[0].shape[1]
    rows = pairs * count
    chip, here = at[0], at[2]
    block = here if early else pl.program_id(0)
    first = block * (8 * pairs) + chip * (2 * pairs)
    turns = [freq[level, 0, low : low + count] for level in range(2)]

    def source(level, k, p):
        return src[level, chip ^ k, 0, pl.ds(first + 2 * p, 1)]

    def raw(block):
        both = block[0].reshape(pairs, 2, count, 128)
        return jnp.concatenate([both[:, 0].reshape(rows, 128), both[:, 1].reshape(rows, 128)], -1)

    left = jnp.concatenate([raw(x[0]), raw(x[1])], 0)
    right = jnp.concatenate([raw(x[2]), raw(x[3])], 0)
    mid = [[None, None], [None, None]]
    for b0 in range(2):
        y = product(left, right, kern0[0, b0])
        for b1 in range(2):
            mid[b0][b1] = jnp.concatenate(
                [
                    packed(
                        y[b1 * rows + p * count : b1 * rows + (p + 1) * count],
                        source(0, 2 * b0 + b1, p) * turns[0],
                    )
                    for p in range(pairs)
                ],
                0,
            )
    left = jnp.concatenate([mid[0][0], mid[1][0]], 0)
    right = jnp.concatenate([mid[0][1], mid[1][1]], 0)
    for b1 in range(2):
        y = product(left, right, kern1[0, b1])
        for b0 in range(2):
            for p in range(pairs):
                outs[2 * b0 + b1][0, p] = packed(
                    y[b0 * rows + p * count : b0 * rows + (p + 1) * count],
                    source(1, 2 * b0 + b1, p) * turns[1],
                )


def level_two(low, count, at, own, other, kern, src, freq, boxes, outs):
    pairs = own[0].shape[1]
    chip = at[0]
    for n in range(own[0].shape[0]):
        part, near, far = boxes(n)
        turns = freq[0, far, low : low + count]
        first = near * (8 * pairs) + chip * (2 * pairs)
        left, right = (
            jnp.concatenate([x[part].reshape(pairs * count, 256) for x in state], 0) for state in (own, other)
        )
        y = product(left, right, kern[0, 0])
        for k in range(4):
            for p in range(pairs):
                row = (k * pairs + p) * count
                angle = src[0, chip ^ k, 0, pl.ds(first + 2 * p, 1)] * turns
                outs(n, k, p, packed(y[row : row + count], angle))


def level_three(low, count, back, at, x, kern, src, freq, outs):
    parts = len(x)
    pairs = x[0].shape[1]
    chip, here = at[0], at[2]
    for q in range(parts // 2):
        left = x[q][...].reshape(4 * pairs * count, 256)
        right = x[q + parts // 2][...].reshape(4 * pairs * count, 256)
        for b in range(2):
            to = here ^ (q + b * (parts // 2))
            turns = freq[0, to, low : low + count]
            y = product(left, right, kern[0, b])
            for k in range(4):
                chunk, near = (chip, chip ^ k) if back else (chip ^ k, chip)
                first = here * (8 * pairs) + near * (2 * pairs)
                for p in range(pairs):
                    row = (k * pairs + p) * count
                    angle = src[0, chunk, 0, pl.ds(first + 2 * p, 1)] * turns
                    outs[k][2 * p, to], outs[k][2 * p + 1, to] = split_pairs(y[row : row + count], angle)


def third_level(low, count, at, *refs):
    own, other, (kern, src, freq), outs = refs[:4], refs[4:8], refs[8:11], refs[11:]
    here = at[2]

    def put(n, k, p, value):
        outs[k][n, p] = value

    level_two(low, count, at, own, other, kern, src, freq, lambda n: (n, n, here), put)


def fourth_level(low, count, at, *refs):
    x, (kern, src, freq), outs = refs[:-7], refs[-7:-4], refs[-4:]
    level_three(low, count, True, at, x, kern, src, freq, outs)


def last_levels(low, count, at, *refs):
    own, other, (kern2, src2, freq2, kern3, src3, freq3) = refs[:4], refs[4:8], refs[8:14]
    outs, held = refs[14:18], refs[18:]
    here = at[2]

    def put(n, k, p, value):
        held[n][k, p] = value

    level_two(low, count, at, own, other, kern2, src2, freq2, lambda n: (n, here, here ^ n), put)
    level_three(low, count, False, at, held, kern3, src3, freq3, outs)


def gather(spans, at, *refs):
    count = 4 * len(spans)
    parts, out, sems = refs[:count], refs[count], refs[count + 1]
    copies = []
    for c, (low, size) in enumerate(spans):
        for k in range(4):
            n = 4 * c + k
            copies.append(
                pltpu.make_async_copy(parts[n], out.at[at[0] ^ k, :, :, pl.ds(low, size)], sems.at[n])
            )
    for copy in copies:
        copy.start()
    for copy in copies:
        copy.wait()


def whole(shape):
    return pl.BlockSpec(shape, lambda *_: (0,) * len(shape))


def call(kernel, at, operands, outs, scratch=(), grid=(1,), in_specs=None, out_specs=None):
    return pl.pallas_call(
        kernel,
        out_shape=outs,
        grid_spec=pltpu.PrefetchScalarGridSpec(
            num_scalar_prefetch=1,
            grid=grid,
            in_specs=in_specs or [whole(x.shape) for x in operands],
            out_specs=out_specs or [whole(x.shape) for x in outs],
            scratch_shapes=list(scratch),
        ),
        compiler_params=pltpu.CompilerParams(vmem_limit_bytes=VMEM),
        cost_estimate=pl.CostEstimate(
            flops=0,
            bytes_accessed=0,
            transcendentals=0,
        ),
    )(at, *operands)


def body(weights, kernels, src_phase, freq_phase):
    n_src, n_freq = lax.axis_size("src"), lax.axis_size("freq")
    src_index, here = lax.axis_index("src"), lax.axis_index("freq")
    s_dev, f_dev, _ = weights.shape
    bits = n_src.bit_length() - 1
    shift = bits - 2
    chip = src_index >> shift
    rest = src_index & ((1 << shift) - 1)
    side = src_index >> (shift - 1) & 1
    near = s_dev // n_freq
    each = near // 4
    pairs = each // 2
    spans = ((0, FIRST), (FIRST, f_dev - FIRST))
    at = jnp.stack([chip, rest, here]).astype(jnp.int32)
    bf16 = jnp.bfloat16

    raw = weights.reshape(n_freq, 4, each, f_dev, 128)

    low, count = spans[0]
    out_a = [
        lax.dynamic_slice(raw, (0, chip ^ k, 0, low, 0), (n_freq, 1, each, count, 128)).reshape(n_freq, each, count, 128)
        for k in range(4)
    ]
    a3 = swapped(out_a[3], "src", 3 << shift)
    a2 = swapped(out_a[2], "src", 2 << shift)
    a1 = swapped(out_a[1], "src", 1 << shift)

    low, count = spans[1]
    out_f = [
        lax.dynamic_slice(raw, (here ^ q, 0, 0, low, 0), (1, 4, each, count, 128)).reshape(4, each, count, 128)
        for q in range(n_freq)
    ]
    moved = [out_f[0]] + [swapped(out_f[q], "freq", q) for q in range(1, n_freq)]
    out_b = [jnp.stack([lax.dynamic_index_in_dim(x, chip ^ k, 0, False) for x in moved], 0) for k in range(4)]
    b3 = swapped(after(out_b[3], a3), "src", 3 << shift)
    b2 = swapped(after(out_b[2], a2), "src", 2 << shift)
    b1 = swapped(after(out_b[1], a1), "src", 1 << shift)

    flips = jnp.stack([chip >> 1, chip & 1, side, here // (n_freq // 2)]).astype(jnp.int32)
    boxes, columns = src_phase.shape[2], freq_phase.shape[2]
    src, freq, wide = call(
        prepare,
        after(flips, out_f[3]),
        [src_phase, freq_phase, kernels],
        [
            jax.ShapeDtypeStruct((4, boxes, 128), jnp.float32),
            jax.ShapeDtypeStruct((4, columns, 128), jnp.float32),
            jax.ShapeDtypeStruct((4, 2, 512, 256), bf16),
        ],
    )
    src = src.reshape(4, 4, 1 << shift, s_dev, 128)
    freq = freq.reshape(4, n_freq, f_dev, 128)

    def tables(level, outputs=2):
        return [
            pl.BlockSpec((1, outputs, 512, 256), lambda *_: (level, 0, 0, 0)),
            pl.BlockSpec((1, 4, 1, s_dev, 128), lambda *a: (level, 0, a[-1][1], 0, 0)),
            pl.BlockSpec((1, n_freq, f_dev, 128), lambda *_: (level, 0, 0, 0)),
        ]

    def levels01(x, span, early):
        low, count = span
        rows = 4 * n_freq * pairs * count
        return call(
            functools.partial(first_levels, low, count, early),
            at,
            [*x, wide, wide, src, freq],
            [jax.ShapeDtypeStruct((n_freq, pairs, count, 256), bf16)] * 4,
            grid=(n_freq,),
            in_specs=[pl.BlockSpec((1, each, count, 128), lambda m, a: (m, 0, 0, 0))] * 4
            + [
                pl.BlockSpec((1, 2, 512, 256), lambda m, a: (0, 0, 0, 0)),
                pl.BlockSpec((1, 2, 512, 256), lambda m, a: (1, 0, 0, 0)),
                pl.BlockSpec((2, 4, 1, s_dev, 128), lambda m, a: (0, 0, a[1], 0, 0)),
                pl.BlockSpec((2, 1, f_dev, 128), lambda m, a: (0, a[2] ^ m if early else a[2], 0, 0)),
            ],
            out_specs=[pl.BlockSpec((1, pairs, count, 256), lambda m, a: (m, 0, 0, 0))] * 4,
        )

    def core(state):
        return [swapped(x, "src", 1 << (shift - 1)) for x in state]

    def back_shapes(count):
        return [jax.ShapeDtypeStruct((each, n_freq, count, 128), bf16)] * 4

    low, count = spans[0]
    state_a = levels01([out_a[0], a1, a2, a3], spans[0], False)
    sent = call(
        functools.partial(third_level, low, count),
        at,
        [*state_a, *core(state_a), wide, src, freq],
        [jax.ShapeDtypeStruct((n_freq, pairs, count, 256), bf16)] * 4,
        in_specs=[whole(state_a[0].shape)] * 8 + tables(2, outputs=1),
    )
    home = [sent[0], None, None, None]
    for k, earlier in ((3, b3), (2, b2), (1, b1)):
        home[k] = swapped(after(sent[k], earlier), "src", k << shift)

    low, count = spans[1]
    state_b = levels01([after(out_b[0], sent[0]), b1, b2, b3], spans[1], True)
    back_b = call(
        functools.partial(last_levels, low, count),
        at,
        [*state_b, *core(state_b), wide, src, freq, wide, src, freq],
        back_shapes(count),
        scratch=[pltpu.VMEM((4, pairs, count, 256), bf16)] * n_freq,
        in_specs=[whole(state_b[0].shape)] * 8 + tables(2, outputs=1) + tables(3),
    )
    end_b = [back_b[0], None, None, None]
    for k in (3, 2, 1):
        end_b[k] = swapped(after(back_b[k], home[k]), "src", k << shift)

    low, count = spans[0]
    home = [after(x, back_b[0]) for x in home]
    cross = [
        jnp.stack([lax.dynamic_index_in_dim(x, here ^ q, 0, False) for x in home], 0) for q in range(n_freq)
    ]
    got = [cross[0]] + [swapped(cross[q], "freq", q) for q in range(1, n_freq)]
    end_a = call(
        functools.partial(fourth_level, low, count),
        at,
        [*got, wide, src, freq],
        back_shapes(count),
        in_specs=[whole(got[0].shape)] * n_freq + tables(3),
    )

    ends = [*end_a, *end_b]
    out = call(
        functools.partial(gather, spans),
        jnp.reshape(chip, (1,)).astype(jnp.int32),
        ends,
        [jax.ShapeDtypeStruct((4, each, n_freq, f_dev, 128), bf16)],
        scratch=[pltpu.SemaphoreType.DMA((len(ends),))],
        in_specs=[pl.BlockSpec(memory_space=pl.ANY)] * len(ends),
        out_specs=[pl.BlockSpec(memory_space=pl.ANY)],
    )[0]
    return out.reshape(near, n_freq * f_dev, 128)


def solution(mesh):
    placed = (P("src", "freq", None), P(), P(), P())
    return jax.shard_map(
        body, mesh=mesh, in_specs=placed, out_specs=P(("src", "freq"), None, None), check_vma=False
    )
```

```python
import functools
import math

import jax
import jax.numpy as jnp
from jax import lax
from jax.experimental import pallas as pl
from jax.experimental.pallas import tpu as pltpu
from jax.sharding import PartitionSpec as P

SIN = (4.44288292, -7.3082457, 3.60635441, -0.84611289, 0.10982699)
COS = (1.4142135, -6.97885099, 5.73946117, -1.88356299, 0.31069819)
NEAREST = 12582912.0
VMEM = 12 * 2**20
FIRST = 64
ORDER = (7, 3, 6, 5, 2, 4, 1, 0)
G_F = {3: (1, (7,))}
G_R = ()
G_A = (7, 6, 5)
G_B = (7, 6, 5)
G_C = {3: (7,)}


def after(value, *earlier):
    return lax.optimization_barrier((value, *earlier))[0]


def turned(u, v, turns):
    part = turns - ((turns + NEAREST) - NEAREST)
    square = part * part
    sine, cosine = SIN[-1], COS[-1]
    for term in SIN[-2::-1]:
        sine = sine * square + term
    for term in COS[-2::-1]:
        cosine = cosine * square + term
    sine = sine * part
    cosine, sine = 1.0 - sine * sine, sine * cosine
    return u * cosine - v * sine, v * cosine + u * sine


def packed(y, turns):
    u, v = turned(y[:, :128], y[:, 128:], turns)
    return jnp.concatenate([u, v], -1).astype(jnp.bfloat16)


def split_pairs(y, turns):
    u, v = turned(y[:, :128], y[:, 128:], turns)
    low = lax.broadcasted_iota(jnp.int32, u.shape, 1) < 64
    first = jnp.where(low, u, pltpu.roll(v, 64, 1))
    second = jnp.where(low, pltpu.roll(u, 64, 1), v)
    return first.astype(jnp.bfloat16), second.astype(jnp.bfloat16)


def product(left, right, kern):
    both = [jnp.concatenate(rows, 0) for rows in (left, right)]
    return jnp.dot(jnp.concatenate(both, -1), kern, preferred_element_type=jnp.float32)


def prepare(spans, parts, at, src_in, freq_in, kern_in, src, src_all, src_home, freq_a, freq_b, wide, held):
    turn = 1.0 / (2.0 * math.pi)
    lanes = lax.broadcasted_iota(jnp.int32, (128, 128), 1) < 64
    group, rest, here = at[0], at[1], at[2]
    each = src.shape[2]
    boxes, columns = src_in.shape[2], freq_in.shape[2]
    s_dev, f_dev = at[3], columns // parts
    for level in range(4):
        rows = src_in[level].T * turn
        held[...] = jnp.concatenate([rows, rows], -1)
        for k in range(8):
            first = ((group ^ k) * (boxes // (8 * s_dev)) + rest) * s_dev + group * each
            for e in range(each):
                src[level, k, pl.ds(e, 1)] = held[pl.ds(first + here * (8 * each) + e, 1)]
                if level == 3:
                    own = (group * (boxes // (8 * s_dev)) + rest) * s_dev + here * (8 * each) + (group ^ k) * each
                    src_home[k, pl.ds(e, 1)] = held[pl.ds(own + e, 1)]
                else:
                    for part in range(parts):
                        src_all[level, k, part, pl.ds(e, 1)] = held[pl.ds(first + part * (8 * each) + e, 1)]
        rows = freq_in[level].T
        for part in range(parts):
            for (low, count), out in zip(spans, (freq_a, freq_b), strict=True):
                base = part * f_dev + low
                half = count // 2
                out[level, part] = jnp.concatenate([rows[base : base + half], rows[base + half : base + count]], -1)
        for b in range(2):
            for c in range(2):
                if level < 3:
                    bit = group >> (2 - level) & 1
                    places = [(level, kern_in[level, b ^ bit, c ^ bit])]
                else:
                    bit = at[4]
                    places = [(3, kern_in[3, b, c]), (4, kern_in[3, b ^ bit, c ^ bit])]
                for place, kern in places:
                    kern = kern.astype(jnp.float32)
                    over = pltpu.roll(kern, 64, 1)
                    none = jnp.zeros_like(kern)
                    forms = [
                        jnp.concatenate([jnp.where(lanes, kern, none), jnp.where(lanes, over, none)], -1),
                        jnp.concatenate([jnp.where(lanes, none, over), jnp.where(lanes, none, kern)], -1),
                    ]
                    for t in range(2):
                        form = forms[t].astype(jnp.bfloat16)
                        if level == 0:
                            wide[place, b, pl.ds(256 * c + 128 * t, 128)] = form
                        else:
                            for ri in range(2):
                                row = 256 * c + 128 * ri + 64 * t
                                wide[place, b, pl.ds(row, 64)] = form[64 * ri : 64 * ri + 64]


def ordered(parts):
    return [parts[ORDER.index(k)] for k in range(8)]


def raw(rows):
    half = rows.shape[0] // 2
    return jnp.concatenate([rows[:half], rows[half:]], -1)


def three_levels(state, tiles, half, wide, angle):
    for level in range(3):
        mask = 4 >> level
        lows = [k for k in range(8) if not k & mask]
        left = [state[k][tile] for k in lows for tile in tiles]
        right = [state[k | mask][tile] for k in lows for tile in tiles]
        new = [None] * 8
        for b in range(2):
            y = product(left, right, wide[level, b])
            for n, k in enumerate(lows):
                to = k | b * mask
                new[to] = {}
                for i, tile in enumerate(tiles):
                    row = (n * len(tiles) + i) * half
                    new[to][tile] = packed(y[row : row + half], angle(level, to, tile))
        state = new
    return state


def all_levels(at, *refs):
    x, (wide, src, freq), outs = ordered(refs[:8]), refs[8:11], refs[11:]
    each, _, _, count, _ = outs[0].shape
    half = count // 2
    tiles = [(part, e) for part in range(2) for e in range(each)]
    state = [{(part, e): raw(x[k][part, 0, e]) for part, e in tiles} for k in range(8)]

    def angle(level, k, tile):
        part, e = tile
        return src[level, k, e : e + 1] * freq[level, part, 0]

    state = three_levels(state, tiles, half, wide, angle)
    keys = [(k, e) for k in range(8) for e in range(each)]
    left = [state[k][0, e] for k, e in keys]
    right = [state[k][1, e] for k, e in keys]
    for part in range(2):
        y = product(left, right, wide[3, part])
        for n, (k, e) in enumerate(keys):
            first, second = split_pairs(y[n * half : n * half + half], angle(3, k, (part, e)))
            outs[k][e, part, 0, :half] = first
            outs[k][e, part, 0, half:] = second


def first_levels(parts, at, *refs):
    x, (wide, src, freq), outs = ordered(refs[:8]), refs[8:11], refs[11:]
    _, each, half, _ = outs[0].shape
    here = at[2]
    tiles = [(part, e) for part in range(parts) for e in range(each)]
    state = [{(part, e): raw(x[k][part, e]) for part, e in tiles} for k in range(8)]

    def angle(level, k, tile):
        part, e = tile
        return src[level, k, part, e : e + 1] * freq[level, here]

    state = three_levels(state, tiles, half, wide, angle)
    for k in range(8):
        for part, e in tiles:
            outs[k][part, e] = state[k][part, e]


def last_level(parts, at, *refs):
    x, (wide, src, freq), outs = refs[:parts], refs[parts : parts + 3], refs[parts + 3 :]
    _, each, half, _ = x[0].shape
    here = at[2]
    keys = [(k, e) for k in range(8) for e in range(each)]
    for q in range(parts // 2):
        left = [x[q][k, e] for k, e in keys]
        right = [x[q + parts // 2][k, e] for k, e in keys]
        for b in range(2):
            to = here ^ (q + b * (parts // 2))
            y = product(left, right, wide[4, b])
            for n, (k, e) in enumerate(keys):
                angle = src[k, e : e + 1] * freq[3, to]
                first, second = split_pairs(y[n * half : n * half + half], angle)
                outs[k][e, to, :half] = first
                outs[k][e, to, half:] = second


def cut_groups(span, at, x, *refs):
    low, count = span
    outs, sems = refs[:-1], refs[-1]
    copies = [
        pltpu.make_async_copy(x.at[:, at[0] ^ k, :, pl.ds(low, count)], out, sems.at[k]) for k, out in enumerate(outs)
    ]
    for copy in copies:
        copy.start()
    for copy in copies:
        copy.wait()


def cut_parts(span, at, x, *refs):
    low, count = span
    outs, sems = refs[:-1], refs[-1]
    copies = [
        pltpu.make_async_copy(x.at[at[2] ^ q, :, :, pl.ds(low, count)], out, sems.at[q]) for q, out in enumerate(outs)
    ]
    for copy in copies:
        copy.start()
    for copy in copies:
        copy.wait()


def regroup(at, *refs):
    outs = refs[-8:]
    for q, x in enumerate(refs[:-8]):
        for k in range(8):
            outs[k][at[2] ^ q] = x[at[0] ^ k]


def regroup_home(at, *refs):
    for k, x in enumerate(ordered(refs[:8])):
        for q, out in enumerate(refs[8:]):
            out[k] = x[at[2] ^ q]


def gather(span, at, *refs):
    parts, out, sems = ordered(refs[:8]), refs[-2], refs[-1]
    low, count = span
    copies = [
        pltpu.make_async_copy(parts[k], out.at[at[0] ^ k, :, :, pl.ds(low, count)], sems.at[k])
        for k in range(8)
    ]
    for copy in copies:
        copy.start()
    for copy in copies:
        copy.wait()


def whole(shape):
    return pl.BlockSpec(shape, lambda *_: (0,) * len(shape))


def call(kernel, at, operands, outs, scratch=(), grid=(1,), in_specs=None, out_specs=None, aliases=None, vmem=VMEM):
    return pl.pallas_call(
        kernel,
        out_shape=outs,
        grid_spec=pltpu.PrefetchScalarGridSpec(
            num_scalar_prefetch=1,
            grid=grid,
            in_specs=in_specs or [whole(x.shape) for x in operands],
            out_specs=out_specs or [whole(x.shape) for x in outs],
            scratch_shapes=list(scratch),
        ),
        input_output_aliases=aliases or {},
        compiler_params=pltpu.CompilerParams(vmem_limit_bytes=vmem),
    )(at, *operands)


def body(weights, kernels, src_phase, freq_phase):
    n_src, n_freq = lax.axis_size("src"), lax.axis_size("freq")
    src_index, here = lax.axis_index("src"), lax.axis_index("freq")
    s_dev, f_dev, _ = weights.shape
    shift = n_src.bit_length() - 4
    group, rest = src_index >> shift, src_index & ((1 << shift) - 1)
    each = s_dev // n_freq // 8
    pairs = n_freq // 2
    first = FIRST * f_dev // 128
    spans = ((0, first), (first, f_dev - first))
    bf16 = jnp.bfloat16
    at = jnp.stack([group, rest, here, jnp.full_like(here, s_dev), here // pairs]).astype(jnp.int32)
    raw_rows = weights.reshape(n_freq, 8, each, f_dev, 128)
    anywhere = pl.BlockSpec(memory_space=pl.ANY)

    def over_src(block, k):
        return lax.ppermute(block, "src", [(i, i ^ k << shift) for i in range(n_src)])

    def over_freq(block, q):
        return lax.ppermute(block, "freq", [(j, j ^ q) for j in range(n_freq)])

    def sent(parts, gates):
        got = [*parts]
        for k in range(1, 8):
            got[k] = over_src(after(parts[k], *gates[k]) if k in gates else parts[k], k)
        return got

    def cut(kernel, span, at, shape, many, vmem):
        return call(
            functools.partial(kernel, span),
            at,
            [raw_rows],
            [jax.ShapeDtypeStruct(shape, bf16)] * many,
            scratch=[pltpu.SemaphoreType.DMA((many,))],
            in_specs=[pl.BlockSpec(memory_space=pltpu.HBM)],
            out_specs=[anywhere] * many,
            vmem=vmem,
        )

    def in_order(parts):
        return [parts[k] for k in ORDER]

    count_a, count_b = first, f_dev - first
    out_a = cut(cut_groups, spans[0], at, (n_freq, each, count_a, 128), 8, VMEM)
    in_a = sent(out_a, {})
    out_f = cut(cut_parts, spans[1], after(at, out_a[0]), (8, each, count_b, 128), n_freq, VMEM)
    src, src_all, src_home, freq_a, freq_b, wide = call(
        functools.partial(prepare, spans, n_freq),
        after(at, out_f[0]),
        [src_phase, freq_phase, kernels],
        [
            jax.ShapeDtypeStruct((4, 8, each, 128), jnp.float32),
            jax.ShapeDtypeStruct((3, 8, n_freq, each, 128), jnp.float32),
            jax.ShapeDtypeStruct((8, each, 128), jnp.float32),
            jax.ShapeDtypeStruct((4, n_freq, count_a // 2, 128), jnp.float32),
            jax.ShapeDtypeStruct((4, n_freq, count_b // 2, 128), jnp.float32),
            jax.ShapeDtypeStruct((5, 2, 512, 256), bf16),
        ],
        scratch=[pltpu.VMEM((src_phase.shape[2], 128), jnp.float32)],
    )
    waits = {q: [wide] * w + [in_a[k] for k in ks] for q, (w, ks) in G_F.items()}
    moved = [out_f[0]] + [
        over_freq(after(out_f[q], *waits[q]) if q in waits else out_f[q], q) for q in range(1, n_freq)
    ]
    out_b = call(regroup, after(at, *[in_a[k] for k in G_R]) if G_R else at, moved, [jax.ShapeDtypeStruct((n_freq, each, count_b, 128), bf16)] * 8)
    in_b = sent(out_b, {})

    back_a = call(
        functools.partial(first_levels, n_freq),
        at,
        [*in_order(in_a), wide, src_all, freq_a],
        [jax.ShapeDtypeStruct((n_freq, each, count_a // 2, 256), bf16)] * 8,
    )
    some = [in_b[k] for k in G_A]
    home = sent(back_a, {k: some for k in range(1, 8)})

    x_spec = pl.BlockSpec((2, 1, each, count_b, 128), lambda n, a: (0, n, 0, 0, 0))
    back_b = call(
        all_levels,
        at,
        [
            *[x.reshape(2, pairs, each, count_b, 128) for x in in_order([after(in_b[0], back_a[0]), *in_b[1:]])],
            wide,
            src,
            freq_b.reshape(4, 2, pairs, count_b // 2, 128),
        ],
        [jax.ShapeDtypeStruct((each, 2, pairs, count_b, 128), bf16)] * 8,
        grid=(pairs,),
        in_specs=[x_spec] * 8
        + [
            whole(wide.shape),
            whole(src.shape),
            pl.BlockSpec((4, 2, 1, count_b // 2, 128), lambda n, a: (0, 0, n, 0, 0)),
        ],
        out_specs=[pl.BlockSpec((each, 2, 1, count_b, 128), lambda n, a: (0, 0, n, 0, 0))] * 8,
    )
    back_b = [x.reshape(each, n_freq, count_b, 128) for x in back_b]
    some = [home[k] for k in G_B]
    end_b = sent(back_b, {k: some for k in range(1, 8)})

    cross = call(
        regroup_home,
        after(at, back_b[0]),
        in_order(home),
        [jax.ShapeDtypeStruct((8, each, count_a // 2, 256), bf16)] * n_freq,
    )
    got = [cross[0]] + [
        over_freq(after(cross[q], *[end_b[k] for k in G_C[q]]) if q in G_C else cross[q], q) for q in range(1, n_freq)
    ]
    end_a = call(
        functools.partial(last_level, n_freq),
        at,
        [*got, wide, src_home, freq_a],
        [jax.ShapeDtypeStruct((each, n_freq, count_a, 128), bf16)] * 8,
    )

    def place(span, parts, out=None):
        operands = in_order(parts) if out is None else [*in_order(parts), out]
        return call(
            functools.partial(gather, span),
            at,
            operands,
            [jax.ShapeDtypeStruct((8, each, n_freq, f_dev, 128), bf16)],
            scratch=[pltpu.SemaphoreType.DMA((8,))],
            in_specs=[anywhere] * len(operands),
            out_specs=[anywhere],
            aliases=None if out is None else {9: 0},
        )[0]

    out = place(spans[0], end_a)
    out = place(spans[1], end_b, out)
    return out.reshape(s_dev // n_freq, n_freq * f_dev, 128)


def solution(mesh):
    placed = (P("src", "freq", None), P(), P(), P())
    return jax.shard_map(
        body, mesh=mesh, in_specs=placed, out_specs=P(("src", "freq"), None, None), check_vma=False
    )
```

```python
import functools
import math

import jax
import jax.numpy as jnp
from jax import lax
from jax.experimental import pallas as pl
from jax.experimental.pallas import tpu as pltpu
from jax.sharding import PartitionSpec as P

SIN = (4.44288292, -7.3082457, 3.60635441, -0.84611289, 0.10982699)
COS = (1.4142135, -6.97885099, 5.73946117, -1.88356299, 0.31069819)
NEAREST = 12582912.0
VMEM = 12 * 2**20
FIRST = 64
ORDER = (6, 3, 7, 5, 2, 4, 1, 0)
ORDER_P = (7, 3, 6, 5, 2, 4, 1, 0)
G_F = {3: (1, (6,))}
G_R = ()
G_A = (7, 6, 5)
G_B = (7, 6, 5)
G_C = {3: (6,)}


def after(value, *earlier):
    return lax.optimization_barrier((value, *earlier))[0]


def turned(u, v, turns):
    part = turns - ((turns + NEAREST) - NEAREST)
    square = part * part
    sine, cosine = SIN[-1], COS[-1]
    for term in SIN[-2::-1]:
        sine = sine * square + term
    for term in COS[-2::-1]:
        cosine = cosine * square + term
    sine = sine * part
    cosine, sine = 1.0 - sine * sine, sine * cosine
    return u * cosine - v * sine, v * cosine + u * sine


def packed(y, turns):
    u, v = turned(y[:, :128], y[:, 128:], turns)
    return jnp.concatenate([u, v], -1).astype(jnp.bfloat16)


def split_pairs(y, turns):
    u, v = turned(y[:, :128], y[:, 128:], turns)
    low = lax.broadcasted_iota(jnp.int32, u.shape, 1) < 64
    first = jnp.where(low, u, pltpu.roll(v, 64, 1))
    second = jnp.where(low, pltpu.roll(u, 64, 1), v)
    return first.astype(jnp.bfloat16), second.astype(jnp.bfloat16)


def product(left, right, kern):
    both = [jnp.concatenate(rows, 0) for rows in (left, right)]
    return jnp.dot(jnp.concatenate(both, -1), kern, preferred_element_type=jnp.float32)


def prepare(spans, parts, at, src_in, freq_in, kern_in, src, src_all, src_home, freq_a, freq_b, wide, held):
    turn = 1.0 / (2.0 * math.pi)
    lanes = lax.broadcasted_iota(jnp.int32, (128, 128), 1) < 64
    group, rest, here = at[0], at[1], at[2]
    each = src.shape[2]
    boxes, columns = src_in.shape[2], freq_in.shape[2]
    s_dev, f_dev = at[3], columns // parts
    for level in range(4):
        rows = src_in[level].T * turn
        held[...] = jnp.concatenate([rows, rows], -1)
        for k in range(8):
            first = ((group ^ k) * (boxes // (8 * s_dev)) + rest) * s_dev + group * each
            for e in range(each):
                src[level, k, pl.ds(e, 1)] = held[pl.ds(first + here * (8 * each) + e, 1)]
                if level == 3:
                    own = (group * (boxes // (8 * s_dev)) + rest) * s_dev + here * (8 * each) + (group ^ k) * each
                    src_home[k, pl.ds(e, 1)] = held[pl.ds(own + e, 1)]
                else:
                    for part in range(parts):
                        src_all[level, k, part, pl.ds(e, 1)] = held[pl.ds(first + part * (8 * each) + e, 1)]
        rows = freq_in[level].T
        for part in range(parts):
            for (low, count), out in zip(spans, (freq_a, freq_b), strict=True):
                base = part * f_dev + low
                half = count // 2
                out[level, part] = jnp.concatenate([rows[base : base + half], rows[base + half : base + count]], -1)
        for b in range(2):
            for c in range(2):
                if level < 3:
                    bit = group >> (2 - level) & 1
                    places = [(level, kern_in[level, b ^ bit, c ^ bit])]
                else:
                    bit = at[4]
                    places = [(3, kern_in[3, b, c]), (4, kern_in[3, b ^ bit, c ^ bit])]
                for place, kern in places:
                    kern = kern.astype(jnp.float32)
                    over = pltpu.roll(kern, 64, 1)
                    none = jnp.zeros_like(kern)
                    forms = [
                        jnp.concatenate([jnp.where(lanes, kern, none), jnp.where(lanes, over, none)], -1),
                        jnp.concatenate([jnp.where(lanes, none, over), jnp.where(lanes, none, kern)], -1),
                    ]
                    for t in range(2):
                        form = forms[t].astype(jnp.bfloat16)
                        if level == 0:
                            wide[place, b, pl.ds(256 * c + 128 * t, 128)] = form
                        else:
                            for ri in range(2):
                                row = 256 * c + 128 * ri + 64 * t
                                wide[place, b, pl.ds(row, 64)] = form[64 * ri : 64 * ri + 64]


def ordered(parts):
    return [parts[ORDER.index(k)] for k in range(8)]


def raw(rows):
    half = rows.shape[0] // 2
    return jnp.concatenate([rows[:half], rows[half:]], -1)


def three_levels(state, tiles, half, wide, angle):
    for level in range(3):
        mask = 4 >> level
        lows = [k for k in range(8) if not k & mask]
        left = [state[k][tile] for k in lows for tile in tiles]
        right = [state[k | mask][tile] for k in lows for tile in tiles]
        new = [None] * 8
        for b in range(2):
            y = product(left, right, wide[level, b])
            for n, k in enumerate(lows):
                to = k | b * mask
                new[to] = {}
                for i, tile in enumerate(tiles):
                    row = (n * len(tiles) + i) * half
                    new[to][tile] = packed(y[row : row + half], angle(level, to, tile))
        state = new
    return state


def all_levels(at, *refs):
    x, (wide, src, freq), outs = ordered(refs[:8]), refs[8:11], refs[11:]
    each, _, _, count, _ = outs[0].shape
    half = count // 2
    tiles = [(part, e) for part in range(2) for e in range(each)]
    state = [{(part, e): raw(x[k][part, 0, e]) for part, e in tiles} for k in range(8)]

    def angle(level, k, tile):
        part, e = tile
        return src[level, k, e : e + 1] * freq[level, part, 0]

    state = three_levels(state, tiles, half, wide, angle)
    keys = [(k, e) for k in range(8) for e in range(each)]
    left = [state[k][0, e] for k, e in keys]
    right = [state[k][1, e] for k, e in keys]
    for part in range(2):
        y = product(left, right, wide[3, part])
        for n, (k, e) in enumerate(keys):
            first, second = split_pairs(y[n * half : n * half + half], angle(3, k, (part, e)))
            outs[k][e, part, 0, :half] = first
            outs[k][e, part, 0, half:] = second


def first_levels(parts, at, *refs):
    x, (wide, src, freq), outs = ordered(refs[:8]), refs[8:11], refs[11:]
    _, each, half, _ = outs[0].shape
    here = at[2]
    tiles = [(part, e) for part in range(parts) for e in range(each)]
    state = [{(part, e): raw(x[k][part, e]) for part, e in tiles} for k in range(8)]

    def angle(level, k, tile):
        part, e = tile
        return src[level, k, part, e : e + 1] * freq[level, here]

    state = three_levels(state, tiles, half, wide, angle)
    for k in range(8):
        for part, e in tiles:
            outs[k][part, e] = state[k][part, e]


def last_level(parts, at, *refs):
    x, (wide, src, freq), outs = refs[:parts], refs[parts : parts + 3], refs[parts + 3 :]
    _, each, half, _ = x[0].shape
    here = at[2]
    keys = [(k, e) for k in range(8) for e in range(each)]
    for q in range(parts // 2):
        left = [x[q][k, e] for k, e in keys]
        right = [x[q + parts // 2][k, e] for k, e in keys]
        for b in range(2):
            to = here ^ (q + b * (parts // 2))
            y = product(left, right, wide[4, b])
            for n, (k, e) in enumerate(keys):
                angle = src[k, e : e + 1] * freq[3, to]
                first, second = split_pairs(y[n * half : n * half + half], angle)
                outs[k][e, to, :half] = first
                outs[k][e, to, half:] = second


def cut_groups(span, at, x, *refs):
    low, count = span
    outs, sems = refs[:-1], refs[-1]
    copies = [
        pltpu.make_async_copy(x.at[:, at[0] ^ k, :, pl.ds(low, count)], out, sems.at[k]) for k, out in enumerate(outs)
    ]
    for copy in copies:
        copy.start()
    for copy in copies:
        copy.wait()


def cut_parts(span, at, x, *refs):
    low, count = span
    outs, sems = refs[:-1], refs[-1]
    copies = [
        pltpu.make_async_copy(x.at[at[2] ^ q, :, :, pl.ds(low, count)], out, sems.at[q]) for q, out in enumerate(outs)
    ]
    for copy in copies:
        copy.start()
    for copy in copies:
        copy.wait()


def regroup(at, *refs):
    outs = refs[-8:]
    for q, x in enumerate(refs[:-8]):
        for k in range(8):
            outs[k][at[2] ^ q] = x[at[0] ^ k]


def regroup_home(at, *refs):
    for k, x in enumerate(ordered(refs[:8])):
        for q, out in enumerate(refs[8:]):
            out[k] = x[at[2] ^ q]


def gather(span, at, *refs):
    parts, out, sems = [refs[ORDER_P.index(k)] for k in range(8)], refs[-2], refs[-1]
    low, count = span
    copies = [
        pltpu.make_async_copy(parts[k], out.at[at[0] ^ k, :, :, pl.ds(low, count)], sems.at[k])
        for k in range(8)
    ]
    for copy in copies:
        copy.start()
    for copy in copies:
        copy.wait()


def whole(shape):
    return pl.BlockSpec(shape, lambda *_: (0,) * len(shape))


def call(kernel, at, operands, outs, scratch=(), grid=(1,), in_specs=None, out_specs=None, aliases=None, vmem=VMEM):
    return pl.pallas_call(
        kernel,
        out_shape=outs,
        grid_spec=pltpu.PrefetchScalarGridSpec(
            num_scalar_prefetch=1,
            grid=grid,
            in_specs=in_specs or [whole(x.shape) for x in operands],
            out_specs=out_specs or [whole(x.shape) for x in outs],
            scratch_shapes=list(scratch),
        ),
        input_output_aliases=aliases or {},
        compiler_params=pltpu.CompilerParams(vmem_limit_bytes=vmem),
    )(at, *operands)


def body(weights, kernels, src_phase, freq_phase):
    n_src, n_freq = lax.axis_size("src"), lax.axis_size("freq")
    src_index, here = lax.axis_index("src"), lax.axis_index("freq")
    s_dev, f_dev, _ = weights.shape
    shift = n_src.bit_length() - 4
    group, rest = src_index >> shift, src_index & ((1 << shift) - 1)
    each = s_dev // n_freq // 8
    pairs = n_freq // 2
    first = FIRST * f_dev // 128
    spans = ((0, first), (first, f_dev - first))
    bf16 = jnp.bfloat16
    at = jnp.stack([group, rest, here, jnp.full_like(here, s_dev), here // pairs]).astype(jnp.int32)
    raw_rows = weights.reshape(n_freq, 8, each, f_dev, 128)
    anywhere = pl.BlockSpec(memory_space=pl.ANY)

    def over_src(block, k):
        return lax.ppermute(block, "src", [(i, i ^ k << shift) for i in range(n_src)])

    def over_freq(block, q):
        return lax.ppermute(block, "freq", [(j, j ^ q) for j in range(n_freq)])

    def sent(parts, gates):
        got = [*parts]
        for k in range(1, 8):
            got[k] = over_src(after(parts[k], *gates[k]) if k in gates else parts[k], k)
        return got

    def cut(kernel, span, at, shape, many, vmem):
        return call(
            functools.partial(kernel, span),
            at,
            [raw_rows],
            [jax.ShapeDtypeStruct(shape, bf16)] * many,
            scratch=[pltpu.SemaphoreType.DMA((many,))],
            in_specs=[pl.BlockSpec(memory_space=pltpu.HBM)],
            out_specs=[anywhere] * many,
            vmem=vmem,
        )

    def in_order(parts):
        return [parts[k] for k in ORDER]

    count_a, count_b = first, f_dev - first
    out_a = cut(cut_groups, spans[0], at, (n_freq, each, count_a, 128), 8, VMEM)
    in_a = sent(out_a, {})
    out_f = cut(cut_parts, spans[1], after(at, out_a[0]), (8, each, count_b, 128), n_freq, VMEM)
    src, src_all, src_home, freq_a, freq_b, wide = call(
        functools.partial(prepare, spans, n_freq),
        after(at, out_f[0]),
        [src_phase, freq_phase, kernels],
        [
            jax.ShapeDtypeStruct((4, 8, each, 128), jnp.float32),
            jax.ShapeDtypeStruct((3, 8, n_freq, each, 128), jnp.float32),
            jax.ShapeDtypeStruct((8, each, 128), jnp.float32),
            jax.ShapeDtypeStruct((4, n_freq, count_a // 2, 128), jnp.float32),
            jax.ShapeDtypeStruct((4, n_freq, count_b // 2, 128), jnp.float32),
            jax.ShapeDtypeStruct((5, 2, 512, 256), bf16),
        ],
        scratch=[pltpu.VMEM((src_phase.shape[2], 128), jnp.float32)],
    )
    waits = {q: [wide] * w + [in_a[k] for k in ks] for q, (w, ks) in G_F.items()}
    moved = [out_f[0]] + [
        over_freq(after(out_f[q], *waits[q]) if q in waits else out_f[q], q) for q in range(1, n_freq)
    ]
    out_b = call(regroup, after(at, *[in_a[k] for k in G_R]) if G_R else at, moved, [jax.ShapeDtypeStruct((n_freq, each, count_b, 128), bf16)] * 8)
    in_b = sent(out_b, {})

    back_a = call(
        functools.partial(first_levels, n_freq),
        at,
        [*in_order(in_a), wide, src_all, freq_a],
        [jax.ShapeDtypeStruct((n_freq, each, count_a // 2, 256), bf16)] * 8,
    )
    some = [in_b[k] for k in G_A]
    home = sent(back_a, {k: some for k in range(1, 8)})

    x_spec = pl.BlockSpec((2, 1, each, count_b, 128), lambda n, a: (0, n, 0, 0, 0))
    back_b = call(
        all_levels,
        at,
        [
            *[x.reshape(2, pairs, each, count_b, 128) for x in in_order([after(in_b[0], back_a[0]), *in_b[1:]])],
            wide,
            src,
            freq_b.reshape(4, 2, pairs, count_b // 2, 128),
        ],
        [jax.ShapeDtypeStruct((each, 2, pairs, count_b, 128), bf16)] * 8,
        grid=(pairs,),
        in_specs=[x_spec] * 8
        + [
            whole(wide.shape),
            whole(src.shape),
            pl.BlockSpec((4, 2, 1, count_b // 2, 128), lambda n, a: (0, 0, n, 0, 0)),
        ],
        out_specs=[pl.BlockSpec((each, 2, 1, count_b, 128), lambda n, a: (0, 0, n, 0, 0))] * 8,
    )
    back_b = [x.reshape(each, n_freq, count_b, 128) for x in back_b]
    some = [home[k] for k in G_B]
    end_b = sent(back_b, {k: some for k in range(1, 8)})

    cross = call(
        regroup_home,
        after(at, back_b[0]),
        in_order(home),
        [jax.ShapeDtypeStruct((8, each, count_a // 2, 256), bf16)] * n_freq,
    )
    got = [cross[0]] + [
        over_freq(after(cross[q], *[end_b[k] for k in G_C[q]]) if q in G_C else cross[q], q) for q in range(1, n_freq)
    ]
    end_a = call(
        functools.partial(last_level, n_freq),
        at,
        [*got, wide, src_home, freq_a],
        [jax.ShapeDtypeStruct((each, n_freq, count_a, 128), bf16)] * 8,
    )

    def place(span, parts, out=None):
        operands = [parts[k] for k in ORDER_P] + ([] if out is None else [out])
        return call(
            functools.partial(gather, span),
            at,
            operands,
            [jax.ShapeDtypeStruct((8, each, n_freq, f_dev, 128), bf16)],
            scratch=[pltpu.SemaphoreType.DMA((8,))],
            in_specs=[anywhere] * len(operands),
            out_specs=[anywhere],
            aliases=None if out is None else {9: 0},
        )[0]

    out = place(spans[0], end_a)
    out = place(spans[1], end_b, out)
    return out.reshape(s_dev // n_freq, n_freq * f_dev, 128)


def solution(mesh):
    placed = (P("src", "freq", None), P(), P(), P())
    return jax.shard_map(
        body, mesh=mesh, in_specs=placed, out_specs=P(("src", "freq"), None, None), check_vma=False
    )
```
